32 devices in a mesh: blk: 2 (over x), tile: 16 (over z, y, core).
Axes of the slice: x: 2, y: 2, z: 4, core: 2. Of those that a mesh axis runs over, the one named last changes fastest.
Arguments:
- forward: float32 [2, 1024, 16384], P(None, 'blk', 'tile'), may hold values from -6 to 6
- backward: float32 [2, 1024, 16384], P(None, 'blk', 'tile'), may hold values from -6 to 6
- phase: float32 [16, 1024], P('tile'), may hold values from -3.140625 to 3.140625
- footprint: int32 [16, 16], P('blk', 'tile'), may hold values 0 or 1
- groups: int32 [1024], replicated, may hold values from 0 to 44
Outputs:
- margin: float32 [2, 1024, 1024], P(None, 'blk', 'tile')
- gradient: float32 [16, 1024], P('tile', 'blk')
The draws below stay inside these ranges and needn't reach their ends.
All inputs are finite; a program needn't handle non-finite values. No bound on the sum of `footprint` on one device may be relied on, other than what follows from the above.
Results may differ from the reference program's by a relative error of at most 0.00016.
Values sent between devices are 32-bit elements; how exact they have to be, the bound alone decides.
A program may use at most 320 MiB of HBM per device.

```python
import math
import jax
import jax.numpy as jnp
from jax import lax

MODES = 1024
WIDTH = 1024
ROWS_DEV = 1
BLOCK = 64
NGROUP = 45
PIX_DEV = 1024
TILES = 16
ROWS = 16
PIXELS = 16384
MODE_BLOCKS = 16


def touch_ends(result, rng, least, high):
    extent = result.shape
    spot = [jax.random.randint(jax.random.fold_in(rng, axis), (), 0, extent[axis]) for axis in range(len(extent))]
    result = result.at[tuple(spot)].set(least)
    longest = extent.index(max(extent))
    spot[longest] = (spot[longest] + 1) % extent[longest]
    return result.at[tuple(spot)].set(high)


def steps_of(own_key, extent, shards, smallest, high):
    loudness, own = 1.0, jax.random.fold_in(own_key, 6)
    for dim, shards_of in shards:
        steps = jnp.exp(jax.random.uniform(jax.random.fold_in(own, dim), (shards_of,), jnp.float32, smallest / len(shards), high / len(shards)))
        loudness = loudness * jnp.repeat(steps, extent[dim] // shards_of).reshape([-1 if axis == dim else 1 for axis in range(len(extent))])
    return loudness


def centred(own_key, shape, deviation, most, shards=(), kind=jnp.bfloat16):
    factor_of = steps_of(own_key, shape, shards, -0.22, 0.18) if shards else 1.0
    result = jax.random.normal(own_key, shape, jnp.float32) * deviation * factor_of
    return jnp.minimum(jnp.maximum(result, -most), most).astype(kind)


def setup_inputs(seed: int = 0) -> dict:
    splits = jax.random.split(jax.random.key(seed), 6)
    forward = centred(splits[0], (2, MODES, PIXELS), 1.0, 6.0, ((1, 2), (2, 16)), jnp.float32)
    backward = centred(splits[1], (2, MODES, PIXELS), 1.0, 6.0, ((1, 2), (2, 16)), jnp.float32)
    phase = jnp.clip(jax.random.uniform(splits[2], (ROWS, WIDTH), jnp.float32, -3.140625, 3.140625), -3.140625, 3.140625)
    footprint = touch_ends((jax.random.randint(splits[3], (MODE_BLOCKS, TILES), 0, 4) < 3).astype(jnp.int32), jax.random.fold_in(splits[3], 1), 0, 1)
    groups = touch_ends(jax.random.randint(splits[4], (MODES,), 0, NGROUP), jax.random.fold_in(splits[4], 1), 0, NGROUP - 1).astype(jnp.int32)
    return dict(forward=forward, backward=backward, phase=phase, footprint=footprint, groups=groups)


highest = lax.Precision.HIGHEST
cross_weight = 0.05

def contract_pixels(left_fields, right_fields):
    return lax.dot_general(left_fields, right_fields, (((1,), (1,)), ((), ())), precision=highest, preferred_element_type=jnp.float32)

def contract_modes(left_fields, right_fields):
    return lax.dot_general(left_fields, right_fields, (((0,), (0,)), ((), ())), precision=highest, preferred_element_type=jnp.float32)

def reference(forward, backward, phase, footprint, groups):
    gate_full = footprint.astype(jnp.float32)
    inverse_root = 1.0 / math.sqrt(PIXELS)

    def tile_fields(tile_index):
        forward_tile = lax.dynamic_slice_in_dim(forward, tile_index * PIX_DEV, PIX_DEV, 2)
        backward_tile = lax.dynamic_slice_in_dim(backward, tile_index * PIX_DEV, PIX_DEV, 2)
        phase_tile = lax.dynamic_slice_in_dim(phase, tile_index * ROWS_DEV, ROWS_DEV, 0).reshape(PIX_DEV)
        gate_rows = jnp.repeat(lax.dynamic_slice_in_dim(gate_full, tile_index, 1, 1)[:, 0], BLOCK)
        masked = backward_tile * gate_rows[None, :, None]
        phase_cos = jnp.cos(phase_tile)
        phase_sin = jnp.sin(phase_tile)
        shifted_re = forward_tile[0] * phase_cos - forward_tile[1] * phase_sin
        shifted_im = forward_tile[0] * phase_sin + forward_tile[1] * phase_cos
        return (masked, shifted_re, shifted_im)

    def add_tile(carry, tile_index):
        masked, shifted_re, shifted_im = tile_fields(tile_index)
        real_part = contract_pixels(masked[0], shifted_re) + contract_pixels(masked[1], shifted_im)
        imag_part = contract_pixels(masked[0], shifted_im) - contract_pixels(masked[1], shifted_re)
        return ((carry[0] + real_part, carry[1] + imag_part), None)
    zero_matrix = jnp.zeros((MODES, MODES), jnp.float32)
    tile_range = jnp.arange(TILES, dtype=jnp.int32)
    (sum_re, sum_im), _ = lax.scan(add_tile, (zero_matrix, zero_matrix), tile_range)
    margin_re = sum_re * inverse_root
    margin_im = sum_im * inverse_root
    same_group = groups[:, None] == groups[None, :]
    weights = jnp.where(same_group, 1.0, -cross_weight).astype(jnp.float32)
    coupled_re = weights * margin_re
    coupled_im = weights * margin_im
    grad_scale = 0.25 / math.sqrt(MODES)

    def grad_tile(tile_index):
        masked, shifted_re, shifted_im = tile_fields(tile_index)
        reply_re = contract_modes(coupled_re, masked[0]) - contract_modes(coupled_im, masked[1])
        reply_im = contract_modes(coupled_re, masked[1]) + contract_modes(coupled_im, masked[0])
        return grad_scale * lax.optimization_barrier(jnp.sum(shifted_im * reply_re - shifted_re * reply_im, axis=0))
    gradient = lax.map(grad_tile, tile_range).reshape(ROWS, WIDTH)
    return (jnp.stack([margin_re, margin_im]), gradient)
```

```python
import math

import jax
import jax.numpy as jnp
from jax import lax
from jax.sharding import PartitionSpec as P

BLOCK = 64
CROSS = 0.05
CHUNKS = 2
HIGH = lax.Precision.HIGH


def pixels_dot(a, b):
    return lax.dot_general(
        a, b, (((1,), (1,)), ((), ())), precision=HIGH, preferred_element_type=jnp.float32
    )


def modes_dot(a, b):
    return lax.dot_general(
        a, b, (((0,), (0,)), ((), ())), precision=HIGH, preferred_element_type=jnp.float32
    )


def pair_margin(masked, fields):
    real = pixels_dot(masked[0], fields[0]) + pixels_dot(masked[1], fields[1])
    imag = pixels_dot(masked[0], fields[1]) - pixels_dot(masked[1], fields[0])
    return jnp.stack([real, imag])


def gradient_part(coupled, masked, fields):
    reply_re = modes_dot(coupled[0], masked[0]) - modes_dot(coupled[1], masked[1])
    reply_im = modes_dot(coupled[0], masked[1]) + modes_dot(coupled[1], masked[0])
    return jnp.sum(fields[1] * reply_re - fields[0] * reply_im, axis=0)


def body(forward, backward, phase, footprint, groups):
    local = backward.shape[1]
    pixels = backward.shape[2]
    modes = groups.shape[0]
    tiles = lax.axis_size("tile")
    share = modes // tiles
    b = lax.axis_index("blk")
    t = lax.axis_index("tile")
    c = jnp.cos(phase)
    s = jnp.sin(phase)
    swap = [(0, 1), (1, 0)]
    size = local // CHUNKS
    pieces, arriving = [], []
    for k in range(CHUNKS):
        f = forward[:, k * size : (k + 1) * size]
        piece = jnp.stack([f[0] * c - f[1] * s, f[0] * s + f[1] * c])
        pieces.append(piece)
        arriving.append(lax.ppermute(piece, "blk", swap))
    gate = jnp.repeat(footprint[:, 0].astype(jnp.float32), BLOCK)
    masked = backward * gate[None, :, None]
    inverse_root = 1.0 / math.sqrt(pixels * tiles)
    turned = jnp.roll(groups, -b * local)
    own_groups = turned[:local]
    margins = []
    own = jnp.concatenate(pieces, axis=1)
    for fields in [own] + arriving:
        part = pair_margin(masked, fields)
        if margins:
            corner = margins[-1][:1, :1, :1]
            part = jnp.where(jnp.isnan(corner), corner, part)
        margins.append(lax.psum(part, "tile"))
    total = jnp.zeros((pixels,), jnp.float32)
    scaled = []
    begin = 0
    for margin, fields in zip(margins, [own] + arriving):
        margin = margin * inverse_root
        scaled.append(margin)
        theirs = turned[begin : begin + fields.shape[1]]
        begin += fields.shape[1]
        weights = jnp.where(own_groups[:, None] == theirs[None, :], 1.0, -CROSS)
        total = total + gradient_part(margin * weights[None], masked, fields)
    whole = jnp.concatenate(scaled, axis=2)
    start = lax.rem(t * share + modes - b * local, modes)
    margin_out = lax.dynamic_slice_in_dim(whole, start, share, 2)
    half = pixels // 2
    halves = total.reshape(1, 2, half)
    mine = lax.dynamic_index_in_dim(halves, b, 1, keepdims=False)
    other = lax.dynamic_index_in_dim(halves, 1 - b, 1, keepdims=False)
    gradient = (mine + lax.ppermute(other, "blk", swap)) * (0.25 / math.sqrt(modes))
    return margin_out, gradient


def solution(mesh):
    placed = (
        P(None, "blk", "tile"),
        P(None, "blk", "tile"),
        P("tile", None),
        P("blk", "tile"),
        P(),
    )
    return jax.shard_map(
        body,
        mesh=mesh,
        in_specs=placed,
        out_specs=(P(None, "blk", "tile"), P("tile", "blk")),
        check_vma=False,
    )
```

```python
import math

import jax
import jax.numpy as jnp
from jax import lax
from jax.sharding import PartitionSpec as P

BLOCK = 64
CROSS = 0.05
PARTS = (1, 1, 1, 1)
HIGH = lax.Precision.HIGH


def pixels_dot(a, b):
    return lax.dot_general(
        a, b, (((1,), (1,)), ((), ())), precision=HIGH, preferred_element_type=jnp.float32
    )


def modes_dot(a, b):
    return lax.dot_general(
        a, b, (((0,), (0,)), ((), ())), precision=HIGH, preferred_element_type=jnp.float32
    )


def pair_margin(masked, fields):
    real = pixels_dot(masked[0], fields[0]) + pixels_dot(masked[1], fields[1])
    imag = pixels_dot(masked[0], fields[1]) - pixels_dot(masked[1], fields[0])
    return jnp.stack([real, imag])


def gradient_part(coupled, masked, fields):
    reply_re = modes_dot(coupled[0], masked[0]) - modes_dot(coupled[1], masked[1])
    reply_im = modes_dot(coupled[0], masked[1]) + modes_dot(coupled[1], masked[0])
    return jnp.sum(fields[1] * reply_re - fields[0] * reply_im, axis=0)


def tile_sum(x, tiles, t):
    steps = [1 << i for i in range(tiles.bit_length() - 1)]
    for step in steps:
        half = x.shape[1] // 2
        bit = lax.rem(t // step, 2)
        pairs = [(i, i ^ step) for i in range(tiles)]
        keep = lax.dynamic_slice_in_dim(x, bit * half, half, 1)
        send = lax.dynamic_slice_in_dim(x, (1 - bit) * half, half, 1)
        x = keep + lax.ppermute(send, "tile", pairs)
    for step in reversed(steps):
        bit = lax.rem(t // step, 2)
        pairs = [(i, i ^ step) for i in range(tiles)]
        got = lax.ppermute(x, "tile", pairs)
        first = jnp.where(bit == 0, x, got)
        second = jnp.where(bit == 0, got, x)
        x = jnp.concatenate([first, second], axis=1)
    return x


def body(forward, backward, phase, footprint, groups):
    local = backward.shape[1]
    pixels = backward.shape[2]
    modes = groups.shape[0]
    tiles = lax.axis_size("tile")
    share = modes // tiles
    b = lax.axis_index("blk")
    t = lax.axis_index("tile")
    c = jnp.cos(phase)
    s = jnp.sin(phase)
    swap = [(0, 1), (1, 0)]
    pieces, arriving = [], []
    top = 0
    for part in PARTS:
        size = local * part // sum(PARTS)
        f = forward[:, top : top + size]
        top += size
        piece = jnp.stack([f[0] * c - f[1] * s, f[0] * s + f[1] * c])
        pieces.append(piece)
        arriving.append(lax.ppermute(piece, "blk", swap))
    gate = jnp.repeat(footprint[:, 0].astype(jnp.float32), BLOCK)
    masked = backward * gate[None, :, None]
    inverse_root = 1.0 / math.sqrt(pixels * tiles)
    turned = jnp.roll(groups, -b * local)
    own_groups = turned[:local]
    margins = []
    own = jnp.concatenate(pieces, axis=1)
    for fields in [own] + arriving:
        margins.append(tile_sum(pair_margin(masked, fields), tiles, t))
    total = jnp.zeros((pixels,), jnp.float32)
    scaled = []
    begin = 0
    for margin, fields in zip(margins, [own] + arriving):
        margin = margin * inverse_root
        scaled.append(margin)
        theirs = turned[begin : begin + fields.shape[1]]
        begin += fields.shape[1]
        weights = jnp.where(own_groups[:, None] == theirs[None, :], 1.0, -CROSS)
        total = total + gradient_part(margin * weights[None], masked, fields)
    whole = jnp.concatenate(scaled, axis=2)
    start = lax.rem(t * share + modes - b * local, modes)
    margin_out = lax.dynamic_slice_in_dim(whole, start, share, 2)
    half = pixels // 2
    halves = total.reshape(1, 2, half)
    mine = lax.dynamic_index_in_dim(halves, b, 1, keepdims=False)
    other = lax.dynamic_index_in_dim(halves, 1 - b, 1, keepdims=False)
    gradient = (mine + lax.ppermute(other, "blk", swap)) * (0.25 / math.sqrt(modes))
    return margin_out, gradient


def solution(mesh):
    placed = (
        P(None, "blk", "tile"),
        P(None, "blk", "tile"),
        P("tile", None),
        P("blk", "tile"),
        P(),
    )
    return jax.shard_map(
        body,
        mesh=mesh,
        in_specs=placed,
        out_specs=(P(None, "blk", "tile"), P("tile", "blk")),
        check_vma=False,
    )
```

```python
import math

import jax
import jax.numpy as jnp
from jax import lax
from jax.sharding import PartitionSpec as P

BLOCK = 64
CROSS = 0.05
PARTS = (1, 1, 1, 1)
GATES = {0: (0,), 2: (1,), 4: (2,), 6: (3,)}
HIGH = lax.Precision.HIGH


def pixels_dot(a, b):
    return lax.dot_general(
        a, b, (((1,), (1,)), ((), ())), precision=HIGH, preferred_element_type=jnp.float32
    )


def modes_dot(a, b):
    return lax.dot_general(
        a, b, (((0,), (0,)), ((), ())), precision=HIGH, preferred_element_type=jnp.float32
    )


def pair_margin(masked, fields):
    real = pixels_dot(masked[0], fields[0]) + pixels_dot(masked[1], fields[1])
    imag = pixels_dot(masked[0], fields[1]) - pixels_dot(masked[1], fields[0])
    return jnp.stack([real, imag])


def gradient_part(coupled, masked, fields):
    reply_re = modes_dot(coupled[0], masked[0]) - modes_dot(coupled[1], masked[1])
    reply_im = modes_dot(coupled[0], masked[1]) + modes_dot(coupled[1], masked[0])
    return jnp.sum(fields[1] * reply_re - fields[0] * reply_im, axis=0)


def tile_sum(x, tiles, t, gates, arriving):
    phase = 0
    for k in gates.get(phase, ()):
        x, arriving[k] = lax.optimization_barrier((x, arriving[k]))
    steps = [1 << i for i in range(tiles.bit_length() - 1)]
    for step in steps:
        half = x.shape[1] // 2
        bit = lax.rem(t // step, 2)
        pairs = [(i, i ^ step) for i in range(tiles)]
        keep = lax.dynamic_slice_in_dim(x, bit * half, half, 1)
        send = lax.dynamic_slice_in_dim(x, (1 - bit) * half, half, 1)
        x = keep + lax.ppermute(send, "tile", pairs)
        phase += 1
        for k in gates.get(phase, ()):
            x, arriving[k] = lax.optimization_barrier((x, arriving[k]))
    for step in reversed(steps):
        bit = lax.rem(t // step, 2)
        pairs = [(i, i ^ step) for i in range(tiles)]
        got = lax.ppermute(x, "tile", pairs)
        first = jnp.where(bit == 0, x, got)
        second = jnp.where(bit == 0, got, x)
        x = jnp.concatenate([first, second], axis=1)
        phase += 1
        for k in gates.get(phase, ()):
            x, arriving[k] = lax.optimization_barrier((x, arriving[k]))
    return x


def body(forward, backward, phase, footprint, groups):
    local = backward.shape[1]
    pixels = backward.shape[2]
    modes = groups.shape[0]
    tiles = lax.axis_size("tile")
    share = modes // tiles
    b = lax.axis_index("blk")
    t = lax.axis_index("tile")
    c = jnp.cos(phase)
    s = jnp.sin(phase)
    swap = [(0, 1), (1, 0)]
    pieces, arriving = [], []
    top = 0
    for part in PARTS:
        size = local * part // sum(PARTS)
        f = forward[:, top : top + size]
        top += size
        piece = jnp.stack([f[0] * c - f[1] * s, f[0] * s + f[1] * c])
        pieces.append(piece)
        arriving.append(lax.ppermute(piece, "blk", swap))
    gate = jnp.repeat(footprint[:, 0].astype(jnp.float32), BLOCK)
    masked = backward * gate[None, :, None]
    inverse_root = 1.0 / math.sqrt(pixels * tiles)
    turned = jnp.roll(groups, -b * local)
    own_groups = turned[:local]
    margins = []
    own = jnp.concatenate(pieces, axis=1)
    margins.append(tile_sum(pair_margin(masked, own), tiles, t, GATES, arriving))
    for fields in arriving:
        margins.append(tile_sum(pair_margin(masked, fields), tiles, t, {}, arriving))
    total = jnp.zeros((pixels,), jnp.float32)
    scaled = []
    begin = 0
    for margin, fields in zip(margins, [own] + arriving):
        margin = margin * inverse_root
        scaled.append(margin)
        theirs = turned[begin : begin + fields.shape[1]]
        begin += fields.shape[1]
        weights = jnp.where(own_groups[:, None] == theirs[None, :], 1.0, -CROSS)
        total = total + gradient_part(margin * weights[None], masked, fields)
    whole = jnp.concatenate(scaled, axis=2)
    start = lax.rem(t * share + modes - b * local, modes)
    margin_out = lax.dynamic_slice_in_dim(whole, start, share, 2)
    half = pixels // 2
    halves = total.reshape(1, 2, half)
    mine = lax.dynamic_index_in_dim(halves, b, 1, keepdims=False)
    other = lax.dynamic_index_in_dim(halves, 1 - b, 1, keepdims=False)
    gradient = (mine + lax.ppermute(other, "blk", swap)) * (0.25 / math.sqrt(modes))
    return margin_out, gradient


def solution(mesh):
    placed = (
        P(None, "blk", "tile"),
        P(None, "blk", "tile"),
        P("tile", None),
        P("blk", "tile"),
        P(),
    )
    return jax.shard_map(
        body,
        mesh=mesh,
        in_specs=placed,
        out_specs=(P(None, "blk", "tile"), P("tile", "blk")),
        check_vma=False,
    )
```

```python
import math

import jax
import jax.numpy as jnp
from jax import lax
from jax.sharding import PartitionSpec as P

BLOCK = 64
CROSS = 0.05
PARTS = (1, 3)
GATES = {0: (0,), 5: (1,)}
HIGH = lax.Precision.HIGH


def pixels_dot(a, b):
    return lax.dot_general(
        a, b, (((1,), (1,)), ((), ())), precision=HIGH, preferred_element_type=jnp.float32
    )


def modes_dot(a, b):
    return lax.dot_general(
        a, b, (((0,), (0,)), ((), ())), precision=HIGH, preferred_element_type=jnp.float32
    )


def pair_margin(masked, fields):
    real = pixels_dot(masked[0], fields[0]) + pixels_dot(masked[1], fields[1])
    imag = pixels_dot(masked[0], fields[1]) - pixels_dot(masked[1], fields[0])
    return jnp.stack([real, imag])


def gradient_part(coupled, masked, fields):
    reply_re = modes_dot(coupled[0], masked[0]) - modes_dot(coupled[1], masked[1])
    reply_im = modes_dot(coupled[0], masked[1]) + modes_dot(coupled[1], masked[0])
    return jnp.sum(fields[1] * reply_re - fields[0] * reply_im, axis=0)


def tile_sum(x, tiles, t, gates, arriving):
    phase = 0
    for k in gates.get(phase, ()):
        x, arriving[k] = lax.optimization_barrier((x, arriving[k]))
    steps = [1 << i for i in range(tiles.bit_length() - 1)]
    for step in steps:
        half = x.shape[1] // 2
        bit = lax.rem(t // step, 2)
        pairs = [(i, i ^ step) for i in range(tiles)]
        keep = lax.dynamic_slice_in_dim(x, bit * half, half, 1)
        send = lax.dynamic_slice_in_dim(x, (1 - bit) * half, half, 1)
        x = keep + lax.ppermute(send, "tile", pairs)
        phase += 1
        for k in gates.get(phase, ()):
            x, arriving[k] = lax.optimization_barrier((x, arriving[k]))
    for step in reversed(steps):
        bit = lax.rem(t // step, 2)
        pairs = [(i, i ^ step) for i in range(tiles)]
        got = lax.ppermute(x, "tile", pairs)
        first = jnp.where(bit == 0, x, got)
        second = jnp.where(bit == 0, got, x)
        x = jnp.concatenate([first, second], axis=1)
        phase += 1
        for k in gates.get(phase, ()):
            x, arriving[k] = lax.optimization_barrier((x, arriving[k]))
    return x


def body(forward, backward, phase, footprint, groups):
    local = backward.shape[1]
    pixels = backward.shape[2]
    modes = groups.shape[0]
    tiles = lax.axis_size("tile")
    share = modes // tiles
    b = lax.axis_index("blk")
    t = lax.axis_index("tile")
    c = jnp.cos(phase)
    s = jnp.sin(phase)
    swap = [(0, 1), (1, 0)]
    pieces, arriving = [], []
    top = 0
    for part in PARTS:
        size = local * part // sum(PARTS)
        f = forward[:, top : top + size]
        top += size
        piece = jnp.stack([f[0] * c - f[1] * s, f[0] * s + f[1] * c])
        pieces.append(piece)
        arriving.append(lax.ppermute(piece, "blk", swap))
    gate = jnp.repeat(footprint[:, 0].astype(jnp.float32), BLOCK)
    masked = backward * gate[None, :, None]
    inverse_root = 1.0 / math.sqrt(pixels * tiles)
    turned = jnp.roll(groups, -b * local)
    own_groups = turned[:local]
    margins = []
    own = jnp.concatenate(pieces, axis=1)
    margins.append(tile_sum(pair_margin(masked, own), tiles, t, GATES, arriving))
    for fields in arriving:
        margins.append(tile_sum(pair_margin(masked, fields), tiles, t, {}, arriving))
    total = jnp.zeros((pixels,), jnp.float32)
    scaled = []
    begin = 0
    for margin, fields in zip(margins, [own] + arriving):
        margin = margin * inverse_root
        scaled.append(margin)
        theirs = turned[begin : begin + fields.shape[1]]
        begin += fields.shape[1]
        weights = jnp.where(own_groups[:, None] == theirs[None, :], 1.0, -CROSS)
        total = total + gradient_part(margin * weights[None], masked, fields)
    whole = jnp.concatenate(scaled, axis=2)
    start = lax.rem(t * share + modes - b * local, modes)
    margin_out = lax.dynamic_slice_in_dim(whole, start, share, 2)
    half = pixels // 2
    halves = total.reshape(1, 2, half)
    mine = lax.dynamic_index_in_dim(halves, b, 1, keepdims=False)
    other = lax.dynamic_index_in_dim(halves, 1 - b, 1, keepdims=False)
    gradient = (mine + lax.ppermute(other, "blk", swap)) * (0.25 / math.sqrt(modes))
    return margin_out, gradient


def solution(mesh):
    placed = (
        P(None, "blk", "tile"),
        P(None, "blk", "tile"),
        P("tile", None),
        P("blk", "tile"),
        P(),
    )
    return jax.shard_map(
        body,
        mesh=mesh,
        in_specs=placed,
        out_specs=(P(None, "blk", "tile"), P("tile", "blk")),
        check_vma=False,
    )
```
